32 devices in a mesh: slab: 8 (over z, y), beam: 4 (over x, core).
Axes of the slice: x: 2, y: 2, z: 4, core: 2. Of those that a mesh axis runs over, the one named last changes fastest.
Arguments:
- traces: bfloat16 [512, 128, 1024], P(('slab', 'beam')), may hold values from -6 to 6
- shot_window: int32 [512], P(('slab', 'beam')), may hold values from 0 to 15, as said below
- trace_slot: int32 [512, 128], P(('slab', 'beam')), may hold values from 0 to 63
- ray_phase: bfloat16 [256, 1024], replicated, may hold values from -0.1875 to 0.1875
- ray_index: int32 [16, 192], P('beam', 'slab'), may hold values from 0 to 255
- beam_basis: bfloat16 [2, 1024, 8192], P(None, 'beam'), may hold values from -0.125 to 0.125
Outputs:
- image: float32 [192, 8192], P('slab', 'beam')
The draws below stay inside these ranges and needn't reach their ends.
Inputs may be any that keep to these rules, and one draw needn't show every extreme that they name: `shot_window`: within each aligned block of 16 shots (the shots of one device), for every beam owner b exactly 4 shots name a window w with w // 4 = b.
All inputs are finite; a program needn't handle non-finite values.
Results may differ from the reference program's by a relative error of at most 0.0041.
Values may be sent and summed in bfloat16 or wider, within the bound.
A program may use at most 64 MiB of HBM per device.

```python
import math
import jax
import jax.numpy as jnp
from jax import lax

NF = 512
P_SIZE = 64
K = 64
WIN_OWN = 4
RAYS = 256
TPS = 128
SH_DEV = 16
LAT = 8192
WINDOWS = 16
SHOTS = 512
NZ = 192


def draw_shot_window(key, part):
    owner_count = WINDOWS // WIN_OWN
    device_count = SHOTS // SH_DEV
    owner_pattern = jnp.tile(jnp.arange(owner_count, dtype=jnp.int32), SH_DEV // owner_count)
    key_list = jax.random.split(jax.random.fold_in(key, 7), device_count)
    shuffled = jax.vmap(lambda single_key: jax.random.permutation(single_key, owner_pattern))(key_list)
    within = jax.random.randint(jax.random.fold_in(key, 11), (device_count, SH_DEV), 0, WIN_OWN)
    return (shuffled * WIN_OWN + within).reshape(SHOTS).astype(jnp.int32)


def set_ends(array, own_key, least, largest):
    longest = array.shape.index(max(array.shape))
    spots = []
    for shift in (0, 1):
        where = [jax.random.randint(jax.random.fold_in(own_key, axis), (), 0, length) for axis, length in enumerate(array.shape)]
        where[longest] = (where[longest] + shift) % array.shape[longest]
        spots.append(tuple(where))
    return array.at[spots[0]].set(least).at[spots[1]].set(largest)


def block_scale(stream_key, shape, cuts, least, high):
    level = 1.0
    for position, blocks in cuts:
        steps = jax.random.uniform(jax.random.fold_in(jax.random.fold_in(stream_key, 6), position), (blocks,), jnp.float32, least / len(cuts), high / len(cuts))
        level = level * jnp.repeat(jnp.exp(steps), shape[position] // blocks).reshape((-1,) + (1,) * (len(shape) - 1 - position))
    return level


def normal_values(key, shape, width, limit, cuts=(), kind=jnp.bfloat16):
    gain = block_scale(key, shape, cuts, -0.22, 0.18) if cuts else 1.0
    result = jax.random.normal(key, shape, jnp.float32) * width * gain
    return jnp.minimum(jnp.maximum(result, -limit), limit).astype(kind)


def setup_inputs(seed: int = 0) -> dict:
    arg_keys = jax.random.split(jax.random.key(seed), 7)
    return {
        "traces": normal_values(arg_keys[0], (SHOTS, TPS, 2 * NF), 1.0, 6.0, ((0, 32),)),
        "shot_window": draw_shot_window(jax.random.fold_in(arg_keys[6], 71), 0),
        "trace_slot": set_ends(jax.random.randint(arg_keys[2], (SHOTS, TPS), 0, K), jax.random.fold_in(arg_keys[2], 1), 0, K - 1).astype(jnp.int32),
        "ray_phase": normal_values(arg_keys[3], (RAYS, 2 * NF), (2 * NF) ** -0.5, 0.1875),
        "ray_index": set_ends(jax.random.randint(arg_keys[4], (WINDOWS, NZ), 0, RAYS), jax.random.fold_in(arg_keys[4], 1), 0, RAYS - 1).astype(jnp.int32),
        "beam_basis": normal_values(arg_keys[5], (2, WINDOWS * P_SIZE, LAT), (2 * WINDOWS * P_SIZE) ** -0.5, 0.125, ((1, 4),)),
    }


def slant_tables():
    phase_steps = (jnp.arange(P_SIZE, dtype=jnp.int32)[:, None] * jnp.arange(K, dtype=jnp.int32)[None, :]) % K
    angles = phase_steps.astype(jnp.float32) * jnp.float32(2.0 * math.pi / K)
    return jnp.cos(angles), jnp.sin(angles)


def slant_stack(binned, cosine_table, sine_table):
    freq_count = binned.shape[-1] // 2
    real_part = binned[..., :freq_count]
    imag_part = binned[..., freq_count:]
    high = lax.Precision.HIGHEST
    panel_re = jnp.einsum("ps,wsf->wpf", cosine_table, real_part, precision=high) + jnp.einsum("ps,wsf->wpf", sine_table, imag_part, precision=high)
    panel_im = jnp.einsum("ps,wsf->wpf", cosine_table, imag_part, precision=high) - jnp.einsum("ps,wsf->wpf", sine_table, real_part, precision=high)
    return jnp.concatenate([panel_re, panel_im], axis=-1)


def reference(traces, shot_window, trace_slot, ray_phase, ray_index, beam_basis):
    block_count = SHOTS // SH_DEV
    trace_blocks = traces.reshape(block_count, SH_DEV * TPS, 2 * NF)
    labels = jnp.repeat(shot_window, TPS) * K + trace_slot.reshape(-1)
    label_blocks = labels.astype(jnp.int32).reshape(block_count, SH_DEV * TPS)

    def accumulate(running, pieces):
        samples, block_labels = pieces
        added = jax.ops.segment_sum(samples.astype(jnp.float32), block_labels, num_segments=WINDOWS * K)
        return running + added, None

    binned, _ = lax.scan(accumulate, jnp.zeros((WINDOWS * K, 2 * NF), jnp.float32), (trace_blocks, label_blocks))
    binned = binned.reshape(WINDOWS, K, 2 * NF)
    cosine_table, sine_table = slant_tables()
    stack_scale = jnp.float32((SHOTS * TPS / WINDOWS) ** -0.5)
    beam_panel = (slant_stack(binned, cosine_table, sine_table) * stack_scale).astype(jnp.bfloat16)
    rays = ray_phase[ray_index]
    panel_re = beam_panel[..., :NF]
    panel_im = beam_panel[..., NF:]
    left_re = jnp.concatenate([panel_re, -panel_im], axis=-1).astype(jnp.float32)
    left_im = jnp.concatenate([panel_im, panel_re], axis=-1).astype(jnp.float32)
    rays_wide = rays.astype(jnp.float32)
    wave_re = jnp.einsum("wzf,wpf->zwp", rays_wide, left_re).astype(jnp.bfloat16)
    wave_im = jnp.einsum("wzf,wpf->zwp", rays_wide, left_im).astype(jnp.bfloat16)
    mixture = jnp.concatenate([wave_re.reshape(NZ, WINDOWS * P_SIZE), -wave_im.reshape(NZ, WINDOWS * P_SIZE)], axis=1)
    basis_rows = beam_basis.reshape(2 * WINDOWS * P_SIZE, LAT)
    return jnp.dot(mixture, basis_rows, preferred_element_type=jnp.float32)
```

```python
import functools

import jax
import jax.numpy as jnp
import numpy as np
from jax import lax
from jax.experimental import pallas as pl
from jax.experimental.pallas import tpu as pltpu
from jax.sharding import PartitionSpec as P

P_SIZE = 64
K = 64
WIN_OWN = 4


def slant_matrix(scale):
    steps = np.arange(K)[:, None] * np.arange(P_SIZE)[None, :] % K
    c = np.cos(2.0 * np.pi * steps / K) * scale
    d = np.sin(2.0 * np.pi * steps / K) * scale
    return np.block([[c, d], [d, -c]]).astype(np.float32)


def wave_kernel(per_step, slabs, window_ref, slot_ref, traces_ref, table_ref, index_ref, out_ref):
    step = pl.program_id(0)

    @pl.when(step == 0)
    def _():
        out_ref[...] = jnp.zeros_like(out_ref)

    traces_per = traces_ref.shape[1]
    half = traces_ref.shape[2] // 2
    rays_n = table_ref.shape[0]
    depths = index_ref.shape[2]
    own = depths // slabs
    ray_rows = lax.broadcasted_iota(jnp.int32, (rays_n, depths), 0)
    slot_rows = lax.broadcasted_iota(jnp.int32, (K, traces_per), 0)
    for t in range(per_step):
        w = window_ref[step * per_step + t]
        pick = (ray_rows == index_ref[w]).astype(jnp.float32).astype(jnp.bfloat16)
        rays = lax.dot_general(
            pick, table_ref[...], (((0,), (0,)), ((), ())), preferred_element_type=jnp.float32
        ).astype(jnp.bfloat16)
        bins = (slot_rows == slot_ref[t]).astype(jnp.float32).astype(jnp.bfloat16)
        binned = jnp.dot(bins, traces_ref[t], preferred_element_type=jnp.float32)
        re, im = binned[:, :half], binned[:, half:]
        both = jnp.concatenate(
            [jnp.concatenate([re, -im], axis=1), jnp.concatenate([im, re], axis=1)], axis=0
        )
        high = both.astype(jnp.bfloat16)
        low = (both - high.astype(jnp.float32)).astype(jnp.bfloat16)
        parts = lax.dot_general(
            rays,
            jnp.concatenate([high, low], axis=0),
            (((1,), (1,)), ((), ())),
            preferred_element_type=jnp.float32,
        )
        part = parts[:, : 2 * K] + parts[:, 2 * K :]
        for s in range(slabs):
            out_ref[s, w] += part[s * own : (s + 1) * own]


def local_waves(traces, shot_window, trace_slot, ray_phase, index_all, slabs):
    shots, per_shot, doubled = traces.shape
    windows, depths = index_all.shape
    per_step = 4 if shots % 4 == 0 else 1
    grid_spec = pltpu.PrefetchScalarGridSpec(
        num_scalar_prefetch=1,
        grid=(shots // per_step,),
        in_specs=[
            pl.BlockSpec((per_step, 1, per_shot), lambda i, w: (i, 0, 0)),
            pl.BlockSpec((per_step, per_shot, doubled), lambda i, w: (i, 0, 0)),
            pl.BlockSpec(ray_phase.shape, lambda i, w: (0, 0)),
            pl.BlockSpec((windows, 1, depths), lambda i, w: (0, 0, 0)),
        ],
        out_specs=pl.BlockSpec((slabs, windows, depths // slabs, 2 * K), lambda i, w: (0, 0, 0, 0)),
    )
    return pl.pallas_call(
        functools.partial(wave_kernel, per_step, slabs),
        out_shape=jax.ShapeDtypeStruct((slabs, windows, depths // slabs, 2 * K), jnp.float32),
        grid_spec=grid_spec,
        compiler_params=pltpu.CompilerParams(vmem_limit_bytes=40 * 1024 * 1024),
        name="local_waves",
    )(
        shot_window,
        trace_slot.reshape(shots, 1, per_shot),
        traces,
        ray_phase,
        index_all.reshape(windows, 1, depths),
    )


def body(traces, shot_window, trace_slot, ray_phase, ray_index, beam_basis):
    shots, per_shot, doubled = traces.shape
    beams = lax.axis_size("beam")
    slabs = lax.axis_size("slab")
    scale = (shots * slabs * beams * per_shot / (WIN_OWN * beams)) ** (-0.5)
    depths = ray_index.shape[1]
    index_all = lax.all_gather(ray_index, ("slab", "beam"))
    index_all = (
        index_all.reshape(slabs, beams, WIN_OWN, depths)
        .transpose(1, 2, 0, 3)
        .reshape(beams * WIN_OWN, slabs * depths)
    )
    waves = local_waves(traces, shot_window, trace_slot, ray_phase, index_all, slabs)
    waves = waves.reshape(slabs, beams, WIN_OWN * depths, 2 * K)
    waves = lax.psum_scatter(waves, "beam", scatter_dimension=1, tiled=False)
    waves = lax.psum_scatter(waves, "slab", scatter_dimension=0, tiled=False)
    wave = jnp.dot(waves, slant_matrix(scale), precision=lax.Precision.HIGHEST)
    wave = wave.reshape(WIN_OWN, depths, 2, P_SIZE).transpose(1, 2, 0, 3)
    mixture = wave.reshape(depths, 2 * WIN_OWN * P_SIZE)
    high = mixture.astype(jnp.bfloat16)
    low = (mixture - high.astype(jnp.float32)).astype(jnp.bfloat16)
    basis_rows = beam_basis.reshape(2 * WIN_OWN * P_SIZE, beam_basis.shape[2])
    both = jnp.dot(
        jnp.concatenate([high, low], axis=0), basis_rows, preferred_element_type=jnp.float32
    )
    image_part = both[:depths] + both[depths:]
    return lax.psum_scatter(image_part, "beam", scatter_dimension=1, tiled=True)


def solution(mesh):
    in_specs = (
        P(("slab", "beam"), None, None),
        P(("slab", "beam")),
        P(("slab", "beam"), None),
        P(),
        P("beam", "slab"),
        P(None, "beam", None),
    )
    out_specs = P("slab", "beam")
    return jax.shard_map(body, mesh=mesh, in_specs=in_specs, out_specs=out_specs, check_vma=False)
```

```python
import functools

import jax
import jax.numpy as jnp
import numpy as np
from jax import lax
from jax.experimental import pallas as pl
from jax.experimental.pallas import tpu as pltpu
from jax.sharding import PartitionSpec as P

P_SIZE = 64
K = 64
WIN_OWN = 4
MESH = pl.DeviceIdType.MESH
F32 = jnp.float32
BF16 = jnp.bfloat16


def slant_matrix(scale):
    steps = np.arange(K)[:, None] * np.arange(P_SIZE)[None, :] % K
    c = np.cos(2.0 * np.pi * steps / K) * scale
    d = np.sin(2.0 * np.pi * steps / K) * scale
    return np.block([[c, d], [d, -c]]).astype(np.float32)


def wave_kernel(per_step, slabs, window_ref, slot_ref, traces_ref, table_ref, index_ref, out_ref):
    step = pl.program_id(0)

    @pl.when(step == 0)
    def _():
        out_ref[...] = jnp.zeros_like(out_ref)

    traces_per = traces_ref.shape[1]
    half = traces_ref.shape[2] // 2
    rays_n = table_ref.shape[0]
    depths = index_ref.shape[2]
    own = depths // slabs
    windows = index_ref.shape[0]
    ray_rows = lax.broadcasted_iota(jnp.int32, (rays_n, depths), 0)
    slot_rows = lax.broadcasted_iota(jnp.int32, (K, traces_per), 0)
    for t in range(per_step):
        w = window_ref[step * per_step + t]
        owner, own_w = w // WIN_OWN, w % WIN_OWN
        place = ((owner % 2) * (windows // (2 * WIN_OWN)) + owner // 2) * WIN_OWN + own_w
        pick = (ray_rows == index_ref[w]).astype(jnp.float32).astype(jnp.bfloat16)
        rays = lax.dot_general(
            pick, table_ref[...], (((0,), (0,)), ((), ())), preferred_element_type=jnp.float32
        ).astype(jnp.bfloat16)
        bins = (slot_rows == slot_ref[t]).astype(jnp.float32).astype(jnp.bfloat16)
        binned = jnp.dot(bins, traces_ref[t], preferred_element_type=jnp.float32)
        re, im = binned[:, :half], binned[:, half:]
        both = jnp.concatenate(
            [jnp.concatenate([re, -im], axis=1), jnp.concatenate([im, re], axis=1)], axis=0
        )
        high = both.astype(jnp.bfloat16)
        low = (both - high.astype(jnp.float32)).astype(jnp.bfloat16)
        parts = lax.dot_general(
            rays,
            jnp.concatenate([high, low], axis=0),
            (((1,), (1,)), ((), ())),
            preferred_element_type=jnp.float32,
        )
        part = parts[:, : 2 * K] + parts[:, 2 * K :]
        for s in range(slabs):
            out_ref[s, place] += part[s * own : (s + 1) * own]


def local_waves(traces, shot_window, trace_slot, ray_phase, index_all, slabs):
    shots, per_shot, doubled = traces.shape
    windows, depths = index_all.shape
    per_step = 4 if shots % 4 == 0 else 1
    grid_spec = pltpu.PrefetchScalarGridSpec(
        num_scalar_prefetch=1,
        grid=(shots // per_step,),
        in_specs=[
            pl.BlockSpec((per_step, 1, per_shot), lambda i, w: (i, 0, 0)),
            pl.BlockSpec((per_step, per_shot, doubled), lambda i, w: (i, 0, 0)),
            pl.BlockSpec(ray_phase.shape, lambda i, w: (0, 0)),
            pl.BlockSpec((windows, 1, depths), lambda i, w: (0, 0, 0)),
        ],
        out_specs=pl.BlockSpec((slabs, windows, depths // slabs, 2 * K), lambda i, w: (0, 0, 0, 0)),
    )
    return pl.pallas_call(
        functools.partial(wave_kernel, per_step, slabs),
        out_shape=jax.ShapeDtypeStruct((slabs, windows, depths // slabs, 2 * K), jnp.float32),
        grid_spec=grid_spec,
        compiler_params=pltpu.CompilerParams(vmem_limit_bytes=40 * 1024 * 1024),
        name="local_waves",
    )(
        shot_window,
        trace_slot.reshape(shots, 1, per_shot),
        traces,
        ray_phase,
        index_all.reshape(windows, 1, depths),
    )


def gather_kernel(slabs, beams, mine_ref, out_ref, held, beam_send, beam_recv, slab_send, slab_recv):
    slab, beam = lax.axis_index("slab"), lax.axis_index("beam")
    beam_peers = [lax.rem(beam + j, beams) for j in range(1, beams)]
    slab_peers = [lax.rem(slab + k, slabs) for k in range(1, slabs)]
    barrier = pltpu.get_barrier_semaphore()
    for b in beam_peers:
        pl.semaphore_signal(barrier, inc=1, device_id=(slab, b), device_id_type=MESH)
    for s in slab_peers:
        pl.semaphore_signal(barrier, inc=1, device_id=(s, beam), device_id_type=MESH)
    held[0, 0] = mine_ref[...]
    pl.semaphore_wait(barrier, beams + slabs - 2)
    copies = []
    for j, b in enumerate(beam_peers):
        copy = pltpu.make_async_remote_copy(
            src_ref=held.at[0, 0],
            dst_ref=held.at[0, j + 1],
            send_sem=beam_send.at[j],
            recv_sem=beam_recv.at[j],
            device_id=(slab, b),
            device_id_type=MESH,
        )
        copy.start()
        copies.append(copy)
    for copy in copies:
        copy.wait()
    copies = []
    for k, s in enumerate(slab_peers):
        copy = pltpu.make_async_remote_copy(
            src_ref=held.at[0],
            dst_ref=held.at[k + 1],
            send_sem=slab_send.at[k],
            recv_sem=slab_recv.at[k],
            device_id=(s, beam),
            device_id_type=MESH,
        )
        copy.start()
        copies.append(copy)
    for copy in copies:
        copy.wait()
    for k in range(slabs):
        for j in range(beams):
            s = lax.rem(slab + slabs - k, slabs)
            b = lax.rem(beam + beams - j, beams)
            out_ref[s, b] = held[k, j]


def gather_index(ray_index, slabs, beams):
    rows, depths = ray_index.shape
    block = (-(-rows // 8) * 8, -(-depths // 128) * 128)
    mine = jnp.pad(ray_index, ((0, block[0] - rows), (0, block[1] - depths)))
    vmem = pl.BlockSpec(memory_space=pltpu.VMEM)
    out = pl.pallas_call(
        functools.partial(gather_kernel, slabs, beams),
        out_shape=jax.ShapeDtypeStruct((slabs, beams) + block, jnp.int32),
        in_specs=[vmem],
        out_specs=vmem,
        scratch_shapes=[
            pltpu.VMEM((slabs, beams) + block, jnp.int32),
            pltpu.SemaphoreType.DMA((beams,)),
            pltpu.SemaphoreType.DMA((beams,)),
            pltpu.SemaphoreType.DMA((slabs,)),
            pltpu.SemaphoreType.DMA((slabs,)),
        ],
        compiler_params=pltpu.CompilerParams(collective_id=0, has_side_effects=True),
        name="gather_index",
    )(mine)
    out = out[:, :, :rows, :depths].transpose(1, 2, 0, 3)
    return out.reshape(beams * rows, slabs * depths)


def image_kernel(
    slabs, chips, waves, slant, basis_hbm, out_ref,
    basis, core_in, chip_out, chip_in, slab_out, slab_in, part_out, part_in, edge_out, edge_in,
    basis_sem, core_s, core_r, chip_s, chip_r, slab_s, slab_r, part_s, part_r, edge_s, edge_r,
):
    slab, beam = lax.axis_index("slab"), lax.axis_index("beam")
    core, chip = lax.rem(beam, 2), lax.div(beam, 2)
    other = 1 - core
    sibling = (slab, 2 * chip + other)
    chip_of = [lax.rem(chip + j, chips) for j in range(chips)]
    slab_of = [lax.rem(slab + k, slabs) for k in range(1, slabs)] + [slab]

    load = pltpu.make_async_copy(basis_hbm, basis, basis_sem)
    load.start()
    barrier = pltpu.get_barrier_semaphore()
    peers = [sibling]
    peers += [(slab, 2 * x + core) for x in chip_of[1:]]
    peers += [(s, beam) for s in slab_of[:-1]]
    for peer in peers:
        pl.semaphore_signal(barrier, inc=1, device_id=peer, device_id_type=MESH)
    pl.semaphore_wait(barrier, len(peers))

    def send(src, dst, send_sem, recv_sem, device):
        copy = pltpu.make_async_remote_copy(
            src_ref=src, dst_ref=dst, send_sem=send_sem, recv_sem=recv_sem,
            device_id=device, device_id_type=MESH,
        )
        copy.start()
        return copy

    sent = []
    core_copies = [
        send(waves.at[s, other], core_in.at[k], core_s.at[k], core_r.at[k], sibling)
        for k, s in enumerate(slab_of)
    ]
    chip_copies = []
    for k, s in enumerate(slab_of):
        core_copies[k].wait_recv()
        row = []
        for j in range(1, chips):
            x = chip_of[j]
            chip_out[k, j - 1] = (waves[s, core, x] + core_in[k, x]).astype(BF16)
            row.append(
                send(
                    chip_out.at[k, j - 1], chip_in.at[k, j - 1],
                    chip_s.at[k, j - 1], chip_r.at[k, j - 1], (slab, 2 * x + core),
                )
            )
        chip_copies.append(row)
    slab_copies = []
    total = None
    for k, s in enumerate(slab_of):
        total = waves[s, core, chip] + core_in[k, chip]
        for j, copy in enumerate(chip_copies[k]):
            copy.wait_recv()
            total = total + chip_in[k, j].astype(F32)
        if k < slabs - 1:
            slab_out[k] = total.astype(BF16)
            slab_copies.append(
                send(slab_out.at[k], slab_in.at[k], slab_s.at[k], slab_r.at[k], (s, beam))
            )
    for k, copy in enumerate(slab_copies):
        copy.wait_recv()
        total = total + slab_in[k].astype(F32)
    wave = jnp.dot(
        total, slant[...], precision=lax.Precision.HIGHEST, preferred_element_type=F32
    )
    depths = out_ref.shape[0]
    lateral = out_ref.shape[1]
    rows = [wave[w * depths : (w + 1) * depths] for w in range(WIN_OWN)]
    mixed = []
    for lo in (0, P_SIZE):
        part = jnp.concatenate([r[:, lo : lo + P_SIZE] for r in rows], axis=1)
        high = part.astype(BF16)
        low = (part - high.astype(F32))
        mixed.append(jnp.concatenate([high.astype(F32), low], axis=0).astype(BF16))
    load.wait()

    def terms(owner):
        cols = pl.ds(pl.multiple_of(owner * lateral, lateral), lateral)
        both = jnp.dot(mixed[0], basis[0, :, cols], preferred_element_type=F32)
        both += jnp.dot(mixed[1], basis[1, :, cols], preferred_element_type=F32)
        return both[:depths] + both[depths:]

    order = list(range(1, chips)) + [0]
    part_copies = {}
    for j in order:
        part_out[j] = terms(2 * chip_of[j] + other)
        part_copies[j] = send(
            part_out.at[j], part_in.at[j], part_s.at[j], part_r.at[j], sibling
        )
    edge_copies = []
    half = lateral // 2
    for j in range(1, chips):
        value = terms(2 * chip_of[j] + core)
        part_copies[j].wait_recv()
        value = value + part_in[j]
        edge_out[j - 1] = jnp.concatenate([value[:, :half], value[:, half:]], axis=0).astype(BF16)
        edge_copies.append(
            send(
                edge_out.at[j - 1], edge_in.at[j - 1], edge_s.at[j - 1], edge_r.at[j - 1],
                (slab, 2 * chip_of[j] + core),
            )
        )
    value = terms(beam)
    part_copies[0].wait_recv()
    out_ref[...] = value + part_in[0]
    for j, copy in enumerate(edge_copies):
        copy.wait_recv()
        edge = edge_in[j].astype(F32)
        out_ref[:, :half] += edge[:depths]
        out_ref[:, half:] += edge[depths:]
    sent = core_copies + slab_copies + list(part_copies.values()) + edge_copies
    for row in chip_copies:
        sent += row
    for copy in sent:
        copy.wait_send()


def sum_and_image(waves, slant, basis, slabs, beams, depths):
    chips = beams // 2
    lateral = basis.shape[2] // beams
    rows = waves.shape[3]
    wide = 2 * K
    hops = max(chips - 1, 1)
    vmem = pl.BlockSpec(memory_space=pltpu.VMEM)
    dma = pltpu.SemaphoreType.DMA
    return pl.pallas_call(
        functools.partial(image_kernel, slabs, chips),
        out_shape=jax.ShapeDtypeStruct((depths, lateral), F32),
        in_specs=[vmem, vmem, pl.BlockSpec(memory_space=pl.ANY)],
        out_specs=vmem,
        scratch_shapes=[
            pltpu.VMEM(basis.shape, BF16),
            pltpu.VMEM((slabs, chips, rows, wide), F32),
            pltpu.VMEM((slabs, hops, rows, wide), BF16),
            pltpu.VMEM((slabs, hops, rows, wide), BF16),
            pltpu.VMEM((slabs, rows, wide), BF16),
            pltpu.VMEM((slabs, rows, wide), BF16),
            pltpu.VMEM((chips, depths, lateral), F32),
            pltpu.VMEM((chips, depths, lateral), F32),
            pltpu.VMEM((hops, 2 * depths, lateral // 2), BF16),
            pltpu.VMEM((hops, 2 * depths, lateral // 2), BF16),
            dma(()),
            dma((slabs,)), dma((slabs,)),
            dma((slabs, hops)), dma((slabs, hops)),
            dma((slabs,)), dma((slabs,)),
            dma((chips,)), dma((chips,)),
            dma((hops,)), dma((hops,)),
        ],
        compiler_params=pltpu.CompilerParams(
            collective_id=1, has_side_effects=True, vmem_limit_bytes=48 * 1024 * 1024
        ),
        name="sum_and_image",
    )(waves, slant, basis)


def body(traces, shot_window, trace_slot, ray_phase, ray_index, beam_basis):
    shots, per_shot, doubled = traces.shape
    beams = lax.axis_size("beam")
    slabs = lax.axis_size("slab")
    scale = (shots * slabs * beams * per_shot / (WIN_OWN * beams)) ** (-0.5)
    depths = ray_index.shape[1]
    index_all = gather_index(ray_index, slabs, beams)
    waves = local_waves(traces, shot_window, trace_slot, ray_phase, index_all, slabs)
    waves = waves.reshape(slabs, 2, beams // 2, WIN_OWN * depths, 2 * K)
    return sum_and_image(waves, slant_matrix(scale), beam_basis, slabs, beams, depths)


def solution(mesh):
    in_specs = (
        P(("slab", "beam"), None, None),
        P(("slab", "beam")),
        P(("slab", "beam"), None),
        P(),
        P("beam", "slab"),
        P(None, "beam", None),
    )
    out_specs = P("slab", "beam")
    return jax.shard_map(body, mesh=mesh, in_specs=in_specs, out_specs=out_specs, check_vma=False)
```

```python
import functools

import jax
import jax.numpy as jnp
import numpy as np
from jax import lax
from jax.experimental import pallas as pl
from jax.experimental.pallas import tpu as pltpu
from jax.sharding import PartitionSpec as P

P_SIZE = 64
K = 64
WIN_OWN = 4
MESH = pl.DeviceIdType.MESH
F32 = jnp.float32
BF16 = jnp.bfloat16


def slant_matrix(scale):
    steps = np.arange(K)[:, None] * np.arange(P_SIZE)[None, :] % K
    c = np.cos(2.0 * np.pi * steps / K) * scale
    d = np.sin(2.0 * np.pi * steps / K) * scale
    return np.block([[c, d], [d, -c]]).astype(np.float32)


def migrate_kernel(
    slabs, beams, window_ref, slot_ref, index_ref, slant, traces_hbm, table_hbm, basis_hbm, out_ref,
    traces, table, basis, order, gathered, index_rows, bins, waves,
    core_in, chip_out, chip_in, slab_out, slab_in, part_out, part_in, edge_out, edge_in,
    table_sem, traces_sem, basis_sem, ib_s, ib_r, is_s, is_r,
    core_s, core_r, chip_s, chip_r, slab_s, slab_r, part_s, part_r, edge_s, edge_r,
):
    chips = beams // 2
    slab, beam = lax.axis_index("slab"), lax.axis_index("beam")
    core, chip = lax.rem(beam, 2), lax.div(beam, 2)
    other = 1 - core
    sibling = (slab, 2 * chip + other)
    chip_of = [lax.rem(chip + j, chips) for j in range(chips)]
    slab_of = [lax.rem(slab + k, slabs) for k in range(1, slabs)] + [slab]
    beam_peers = [(slab, lax.rem(beam + j, beams)) for j in range(1, beams)]
    slab_peers = [(s, beam) for s in slab_of[:-1]]

    load_table = pltpu.make_async_copy(table_hbm, table, table_sem)
    load_traces = pltpu.make_async_copy(traces_hbm, traces, traces_sem)
    load_basis = pltpu.make_async_copy(basis_hbm, basis, basis_sem)
    load_traces.start()
    load_table.start()
    barrier = pltpu.get_barrier_semaphore()
    for peer in beam_peers + slab_peers:
        pl.semaphore_signal(barrier, inc=1, device_id=peer, device_id_type=MESH)

    def send(src, dst, send_sem, recv_sem, device):
        copy = pltpu.make_async_remote_copy(
            src_ref=src, dst_ref=dst, send_sem=send_sem, recv_sem=recv_sem,
            device_id=device, device_id_type=MESH,
        )
        copy.start()
        return copy

    own_rows, depths = index_ref.shape
    gathered[slab, beam] = jnp.zeros(gathered.shape[2:], jnp.int32)
    gathered[slab, beam, :own_rows, :depths] = index_ref[...]
    shots, per_shot, doubled = traces.shape
    per_owner = shots // beams
    counts = [jnp.int32(0)] * beams
    places = []
    for i in range(shots):
        owner = lax.div(window_ref[i], WIN_OWN)
        place = jnp.int32(0)
        for b in range(beams):
            hit = owner == b
            place = jnp.where(hit, b * per_owner + counts[b], place)
            counts[b] = jnp.where(hit, counts[b] + 1, counts[b])
        places.append(place)
    for m in range(shots):
        shot = jnp.int32(0)
        for i in range(shots):
            shot = jnp.where(places[i] == m, jnp.int32(i), shot)
        order[m] = shot
    pl.semaphore_wait(barrier, len(beam_peers) + len(slab_peers))
    first = [
        send(gathered.at[slab, beam], gathered.at[slab, beam], ib_s.at[j], ib_r.at[j], peer)
        for j, peer in enumerate(beam_peers)
    ]

    half_f = doubled // 2
    slot_rows = lax.broadcasted_iota(jnp.int32, (K, per_shot), 0)

    def bin_shot(m, carry):
        shot = order[m]
        pick = (slot_rows == slot_ref[shot]).astype(F32).astype(BF16)
        binned = jnp.dot(pick, traces[shot], preferred_element_type=F32)
        re, im = binned[:, :half_f], binned[:, half_f:]
        both = jnp.concatenate(
            [jnp.concatenate([re, -im], axis=1), jnp.concatenate([im, re], axis=1)], axis=0
        )
        high = both.astype(BF16)
        bins[m, : 2 * K] = high
        bins[m, 2 * K :] = (both - high.astype(F32)).astype(BF16)
        return carry

    load_traces.wait()
    load_basis.start()
    lax.fori_loop(0, shots // 2, bin_shot, 0, unroll=2)
    for copy in first:
        copy.wait()
    second = [
        send(gathered.at[slab], gathered.at[slab], is_s.at[k], is_r.at[k], peer)
        for k, peer in enumerate(slab_peers)
    ]
    lax.fori_loop(shots // 2, shots, bin_shot, 0, unroll=2)
    load_table.wait()
    for copy in second:
        copy.wait()
    for b in range(beams):
        line = jnp.concatenate([gathered[s, b][:own_rows, :depths] for s in range(slabs)], axis=1)
        for w in range(WIN_OWN):
            index_rows[b * WIN_OWN + w] = line[w : w + 1]

    ray_rows = lax.broadcasted_iota(jnp.int32, (table.shape[0], slabs * depths), 0)

    def owner_waves(x, c):
        owner = 2 * x + c
        waves[c, x] = jnp.zeros(waves.shape[2:], F32)

        def one(t, carry):
            m = owner * per_owner + t
            w = window_ref[order[m]]
            pick = (ray_rows == index_rows[w]).astype(F32).astype(BF16)
            rays = lax.dot_general(
                pick, table[...], (((0,), (0,)), ((), ())), preferred_element_type=F32
            ).astype(BF16)
            parts = lax.dot_general(
                rays, bins[m], (((1,), (1,)), ((), ())), preferred_element_type=F32
            )
            part = parts[:, : 2 * K] + parts[:, 2 * K :]
            for v in range(WIN_OWN):
                weight = jnp.where(w == owner * WIN_OWN + v, 1.0, 0.0)
                for s in range(slabs):
                    waves[c, x, s, v * depths : (v + 1) * depths, :] += (
                        weight * part[s * depths : (s + 1) * depths]
                    )
            return carry

        lax.fori_loop(0, per_owner, one, 0, unroll=2)

    core_copies = {}
    chip_copies = [[] for _ in slab_of]
    for j in list(range(1, chips)) + [0]:
        x = chip_of[j]
        owner_waves(x, other)
        core_copies[j] = send(
            waves.at[other, x], core_in.at[j], core_s.at[j], core_r.at[j], sibling
        )
        owner_waves(x, core)
        core_copies[j].wait_recv()
        if j == 0:
            continue
        for k, s in enumerate(slab_of):
            chip_out[k, j - 1] = (waves[core, x, s] + core_in[j, s]).astype(BF16)
            chip_copies[k].append(
                send(
                    chip_out.at[k, j - 1], chip_in.at[k, j - 1],
                    chip_s.at[k, j - 1], chip_r.at[k, j - 1], (slab, 2 * x + core),
                )
            )
    slab_copies = []
    total = None
    for k, s in enumerate(slab_of):
        total = waves[core, chip, s] + core_in[0, s]
        for j, copy in enumerate(chip_copies[k]):
            copy.wait_recv()
            total = total + chip_in[k, j].astype(F32)
        if k < slabs - 1:
            slab_out[k] = total.astype(BF16)
            slab_copies.append(
                send(slab_out.at[k], slab_in.at[k], slab_s.at[k], slab_r.at[k], (s, beam))
            )
    for k, copy in enumerate(slab_copies):
        copy.wait_recv()
        total = total + slab_in[k].astype(F32)
    wave = jnp.dot(
        total, slant[...], precision=lax.Precision.HIGHEST, preferred_element_type=F32
    )
    lateral = out_ref.shape[1]
    rows = [wave[w * depths : (w + 1) * depths] for w in range(WIN_OWN)]
    mixed = []
    for lo in (0, P_SIZE):
        part = jnp.concatenate([r[:, lo : lo + P_SIZE] for r in rows], axis=1)
        high = part.astype(BF16)
        low = (part - high.astype(F32))
        mixed.append(jnp.concatenate([high.astype(F32), low], axis=0).astype(BF16))
    load_basis.wait()

    def terms(owner):
        cols = pl.ds(pl.multiple_of(owner * lateral, lateral), lateral)
        both = jnp.dot(mixed[0], basis[0, :, cols], preferred_element_type=F32)
        both += jnp.dot(mixed[1], basis[1, :, cols], preferred_element_type=F32)
        return both[:depths] + both[depths:]

    order = list(range(1, chips)) + [0]
    part_copies = {}
    for j in order:
        part_out[j] = terms(2 * chip_of[j] + other)
        part_copies[j] = send(
            part_out.at[j], part_in.at[j], part_s.at[j], part_r.at[j], sibling
        )
    edge_copies = []
    half = lateral // 2
    for j in range(1, chips):
        value = terms(2 * chip_of[j] + core)
        part_copies[j].wait_recv()
        value = value + part_in[j]
        edge_out[j - 1] = jnp.concatenate([value[:, :half], value[:, half:]], axis=0).astype(BF16)
        edge_copies.append(
            send(
                edge_out.at[j - 1], edge_in.at[j - 1], edge_s.at[j - 1], edge_r.at[j - 1],
                (slab, 2 * chip_of[j] + core),
            )
        )
    value = terms(beam)
    part_copies[0].wait_recv()
    out_ref[...] = value + part_in[0]
    for j, copy in enumerate(edge_copies):
        copy.wait_recv()
        edge = edge_in[j].astype(F32)
        out_ref[:, :half] += edge[:depths]
        out_ref[:, half:] += edge[depths:]
    sent = list(core_copies.values()) + slab_copies + list(part_copies.values()) + edge_copies
    for row in chip_copies:
        sent += row
    for copy in sent:
        copy.wait_send()


def body(traces, shot_window, trace_slot, ray_phase, ray_index, beam_basis):
    shots, per_shot, doubled = traces.shape
    beams = lax.axis_size("beam")
    slabs = lax.axis_size("slab")
    scale = (shots * slabs * beams * per_shot / (WIN_OWN * beams)) ** (-0.5)
    own_rows, depths = ray_index.shape
    chips = beams // 2
    lateral = beam_basis.shape[2] // beams
    rows = WIN_OWN * depths
    wide = 2 * K
    hops = max(chips - 1, 1)
    vmem = pl.BlockSpec(memory_space=pltpu.VMEM)
    smem = pl.BlockSpec(memory_space=pltpu.SMEM)
    hbm = pl.BlockSpec(memory_space=pl.ANY)
    dma = pltpu.SemaphoreType.DMA
    block = (-(-own_rows // 8) * 8, -(-depths // 128) * 128)
    return pl.pallas_call(
        functools.partial(migrate_kernel, slabs, beams),
        out_shape=jax.ShapeDtypeStruct((depths, lateral), F32),
        in_specs=[smem, vmem, vmem, vmem, hbm, hbm, hbm],
        out_specs=vmem,
        scratch_shapes=[
            pltpu.VMEM(traces.shape, BF16),
            pltpu.VMEM(ray_phase.shape, BF16),
            pltpu.VMEM(beam_basis.shape, BF16),
            pltpu.SMEM((shots,), jnp.int32),
            pltpu.VMEM((slabs, beams) + block, jnp.int32),
            pltpu.VMEM((beams * WIN_OWN, 1, slabs * depths), jnp.int32),
            pltpu.VMEM((shots, 4 * K, doubled), BF16),
            pltpu.VMEM((2, chips, slabs, rows, wide), F32),
            pltpu.VMEM((chips, slabs, rows, wide), F32),
            pltpu.VMEM((slabs, hops, rows, wide), BF16),
            pltpu.VMEM((slabs, hops, rows, wide), BF16),
            pltpu.VMEM((slabs, rows, wide), BF16),
            pltpu.VMEM((slabs, rows, wide), BF16),
            pltpu.VMEM((chips, depths, lateral), F32),
            pltpu.VMEM((chips, depths, lateral), F32),
            pltpu.VMEM((hops, 2 * depths, lateral // 2), BF16),
            pltpu.VMEM((hops, 2 * depths, lateral // 2), BF16),
            dma(()), dma(()), dma(()),
            dma((beams,)), dma((beams,)),
            dma((slabs,)), dma((slabs,)),
            dma((chips,)), dma((chips,)),
            dma((slabs, hops)), dma((slabs, hops)),
            dma((slabs,)), dma((slabs,)),
            dma((chips,)), dma((chips,)),
            dma((hops,)), dma((hops,)),
        ],
        compiler_params=pltpu.CompilerParams(
            collective_id=0, has_side_effects=True, vmem_limit_bytes=56 * 1024 * 1024
        ),
        name="migrate",
    )(
        shot_window, trace_slot.reshape(shots, 1, per_shot), ray_index, slant_matrix(scale),
        traces, ray_phase, beam_basis,
    )


def solution(mesh):
    in_specs = (
        P(("slab", "beam"), None, None),
        P(("slab", "beam")),
        P(("slab", "beam"), None),
        P(),
        P("beam", "slab"),
        P(None, "beam", None),
    )
    out_specs = P("slab", "beam")
    return jax.shard_map(body, mesh=mesh, in_specs=in_specs, out_specs=out_specs, check_vma=False)
```

```python
import functools

import jax
import jax.numpy as jnp
import numpy as np
from jax import lax
from jax.experimental import pallas as pl
from jax.experimental.pallas import tpu as pltpu
from jax.sharding import PartitionSpec as P

P_SIZE = 64
K = 64
WIN_OWN = 4
MESH = pl.DeviceIdType.MESH
F32 = jnp.float32
BF16 = jnp.bfloat16


def slant_matrix(scale):
    steps = np.arange(K)[:, None] * np.arange(P_SIZE)[None, :] % K
    c = np.cos(2.0 * np.pi * steps / K) * scale
    d = np.sin(2.0 * np.pi * steps / K) * scale
    return np.block([[c, d], [d, -c]]).astype(np.float32)


def migrate_kernel(
    slabs, beams, window_ref, slot_ref, index_ref, slant, traces_hbm, table_hbm, basis_hbm, out_ref,
    traces, table, basis, order, gathered, index_rows, products, waves,
    core_in, chip_out, chip_in, slab_out, slab_in, part_out, part_in, edge_out, edge_in,
    table_sem, traces_sem, basis_sem, ib_s, ib_r, is_s, is_r,
    core_s, core_r, chip_s, chip_r, slab_s, slab_r, part_s, part_r, edge_s, edge_r,
):
    chips = beams // 2
    slab, beam = lax.axis_index("slab"), lax.axis_index("beam")
    core, chip = lax.rem(beam, 2), lax.div(beam, 2)
    other = 1 - core
    sibling = (slab, 2 * chip + other)
    chip_of = [lax.rem(chip + j, chips) for j in range(chips)]
    slab_of = [lax.rem(slab + k, slabs) for k in range(1, slabs)] + [slab]
    beam_peers = [(slab, lax.rem(beam + j, beams)) for j in range(1, beams)]
    slab_peers = [(s, beam) for s in slab_of[:-1]]

    load_table = pltpu.make_async_copy(table_hbm, table, table_sem)
    load_traces = pltpu.make_async_copy(traces_hbm, traces, traces_sem)
    load_basis = pltpu.make_async_copy(basis_hbm, basis, basis_sem)
    load_traces.start()
    load_table.start()
    barrier = pltpu.get_barrier_semaphore()
    for peer in beam_peers + slab_peers:
        pl.semaphore_signal(barrier, inc=1, device_id=peer, device_id_type=MESH)

    def send(src, dst, send_sem, recv_sem, device):
        copy = pltpu.make_async_remote_copy(
            src_ref=src, dst_ref=dst, send_sem=send_sem, recv_sem=recv_sem,
            device_id=device, device_id_type=MESH,
        )
        copy.start()
        return copy

    own_rows, depths = index_ref.shape
    gathered[slab, beam] = jnp.zeros(gathered.shape[2:], jnp.int32)
    gathered[slab, beam, :own_rows, :depths] = index_ref[...]
    shots, per_shot, doubled = traces.shape
    per_owner = shots // beams
    counts = [jnp.int32(0)] * beams
    places = []
    for i in range(shots):
        owner = lax.div(window_ref[i], WIN_OWN)
        place = jnp.int32(0)
        for b in range(beams):
            hit = owner == b
            place = jnp.where(hit, b * per_owner + counts[b], place)
            counts[b] = jnp.where(hit, counts[b] + 1, counts[b])
        places.append(place)
    for m in range(shots):
        shot = jnp.int32(0)
        for i in range(shots):
            shot = jnp.where(places[i] == m, jnp.int32(i), shot)
        order[m] = shot
    pl.semaphore_wait(barrier, len(beam_peers) + len(slab_peers))
    first = [
        send(gathered.at[slab, beam], gathered.at[slab, beam], ib_s.at[j], ib_r.at[j], peer)
        for j, peer in enumerate(beam_peers)
    ]

    half_f = doubled // 2
    slot_rows = lax.broadcasted_iota(jnp.int32, (K, per_shot), 0)

    def bin_shot(m, carry):
        shot = order[m]
        pick = (slot_rows == slot_ref[shot]).astype(F32).astype(BF16)
        binned = jnp.dot(pick, traces[shot], preferred_element_type=F32)
        re, im = binned[:, :half_f], binned[:, half_f:]
        both = jnp.concatenate(
            [jnp.concatenate([re, -im], axis=1), jnp.concatenate([im, re], axis=1)], axis=0
        )
        high = both.astype(BF16)
        low = (both - high.astype(F32)).astype(BF16)
        parts = lax.dot_general(
            table[...],
            jnp.concatenate([high, low], axis=0),
            (((1,), (1,)), ((), ())),
            preferred_element_type=F32,
        )
        part = parts[:, : 2 * K] + parts[:, 2 * K :]
        base = lax.div(m, per_owner) * WIN_OWN
        for v in range(WIN_OWN):
            weight = jnp.where(window_ref[shot] == base + v, 1.0, 0.0)
            products[base + v] += weight * part
        return carry

    products[...] = jnp.zeros(products.shape, F32)
    load_table.wait()
    load_traces.wait()
    load_basis.start()
    lax.fori_loop(0, shots // 2, bin_shot, 0, unroll=4)
    for copy in first:
        copy.wait()
    second = [
        send(gathered.at[slab], gathered.at[slab], is_s.at[k], is_r.at[k], peer)
        for k, peer in enumerate(slab_peers)
    ]
    lax.fori_loop(shots // 2, shots, bin_shot, 0, unroll=4)
    for copy in second:
        copy.wait()
    for b in range(beams):
        line = jnp.concatenate([gathered[s, b][:own_rows, :depths] for s in range(slabs)], axis=1)
        for w in range(WIN_OWN):
            index_rows[b * WIN_OWN + w] = line[w : w + 1]

    ray_rows = lax.broadcasted_iota(jnp.int32, (table.shape[0], slabs * depths), 0)

    def owner_waves(x, c):
        owner = 2 * x + c
        for v in range(WIN_OWN):
            w = owner * WIN_OWN + v
            pick = (ray_rows == index_rows[w]).astype(F32).astype(BF16)
            value = products[w]
            high = value.astype(BF16)
            low = (value - high.astype(F32)).astype(BF16)
            parts = lax.dot_general(
                pick,
                jnp.concatenate([high, low], axis=1),
                (((0,), (0,)), ((), ())),
                preferred_element_type=F32,
            )
            part = parts[:, : 2 * K] + parts[:, 2 * K :]
            for s in range(slabs):
                waves[c, x, s, v * depths : (v + 1) * depths, :] = (
                    part[s * depths : (s + 1) * depths]
                )

    core_copies = {}
    chip_copies = [[] for _ in slab_of]
    for j in list(range(1, chips)) + [0]:
        x = chip_of[j]
        owner_waves(x, other)
        core_copies[j] = send(
            waves.at[other, x], core_in.at[j], core_s.at[j], core_r.at[j], sibling
        )
        owner_waves(x, core)
        core_copies[j].wait_recv()
        if j == 0:
            continue
        for k, s in enumerate(slab_of):
            chip_out[k, j - 1] = (waves[core, x, s] + core_in[j, s]).astype(BF16)
            chip_copies[k].append(
                send(
                    chip_out.at[k, j - 1], chip_in.at[k, j - 1],
                    chip_s.at[k, j - 1], chip_r.at[k, j - 1], (slab, 2 * x + core),
                )
            )
    slab_copies = []
    total = None
    for k, s in enumerate(slab_of):
        total = waves[core, chip, s] + core_in[0, s]
        for j, copy in enumerate(chip_copies[k]):
            copy.wait_recv()
            total = total + chip_in[k, j].astype(F32)
        if k < slabs - 1:
            slab_out[k] = total.astype(BF16)
            slab_copies.append(
                send(slab_out.at[k], slab_in.at[k], slab_s.at[k], slab_r.at[k], (s, beam))
            )
    for k, copy in enumerate(slab_copies):
        copy.wait_recv()
        total = total + slab_in[k].astype(F32)
    wave = jnp.dot(
        total, slant[...], precision=lax.Precision.HIGHEST, preferred_element_type=F32
    )
    lateral = out_ref.shape[1]
    rows = [wave[w * depths : (w + 1) * depths] for w in range(WIN_OWN)]
    mixed = []
    for lo in (0, P_SIZE):
        part = jnp.concatenate([r[:, lo : lo + P_SIZE] for r in rows], axis=1)
        high = part.astype(BF16)
        low = (part - high.astype(F32))
        mixed.append(jnp.concatenate([high.astype(F32), low], axis=0).astype(BF16))
    load_basis.wait()

    def terms(owner):
        cols = pl.ds(pl.multiple_of(owner * lateral, lateral), lateral)
        both = jnp.dot(mixed[0], basis[0, :, cols], preferred_element_type=F32)
        both += jnp.dot(mixed[1], basis[1, :, cols], preferred_element_type=F32)
        return both[:depths] + both[depths:]

    order = list(range(1, chips)) + [0]
    part_copies = {}
    for j in order:
        part_out[j] = terms(2 * chip_of[j] + other)
        part_copies[j] = send(
            part_out.at[j], part_in.at[j], part_s.at[j], part_r.at[j], sibling
        )
    edge_copies = []
    half = lateral // 2
    for j in range(1, chips):
        value = terms(2 * chip_of[j] + core)
        part_copies[j].wait_recv()
        value = value + part_in[j]
        edge_out[j - 1] = jnp.concatenate([value[:, :half], value[:, half:]], axis=0).astype(BF16)
        edge_copies.append(
            send(
                edge_out.at[j - 1], edge_in.at[j - 1], edge_s.at[j - 1], edge_r.at[j - 1],
                (slab, 2 * chip_of[j] + core),
            )
        )
    value = terms(beam)
    part_copies[0].wait_recv()
    out_ref[...] = value + part_in[0]
    for j, copy in enumerate(edge_copies):
        copy.wait_recv()
        edge = edge_in[j].astype(F32)
        out_ref[:, :half] += edge[:depths]
        out_ref[:, half:] += edge[depths:]
    sent = list(core_copies.values()) + slab_copies + list(part_copies.values()) + edge_copies
    for row in chip_copies:
        sent += row
    for copy in sent:
        copy.wait_send()


def body(traces, shot_window, trace_slot, ray_phase, ray_index, beam_basis):
    shots, per_shot, doubled = traces.shape
    beams = lax.axis_size("beam")
    slabs = lax.axis_size("slab")
    scale = (shots * slabs * beams * per_shot / (WIN_OWN * beams)) ** (-0.5)
    own_rows, depths = ray_index.shape
    chips = beams // 2
    lateral = beam_basis.shape[2] // beams
    rows = WIN_OWN * depths
    wide = 2 * K
    hops = max(chips - 1, 1)
    vmem = pl.BlockSpec(memory_space=pltpu.VMEM)
    smem = pl.BlockSpec(memory_space=pltpu.SMEM)
    hbm = pl.BlockSpec(memory_space=pl.ANY)
    dma = pltpu.SemaphoreType.DMA
    block = (-(-own_rows // 8) * 8, -(-depths // 128) * 128)
    return pl.pallas_call(
        functools.partial(migrate_kernel, slabs, beams),
        out_shape=jax.ShapeDtypeStruct((depths, lateral), F32),
        in_specs=[smem, vmem, vmem, vmem, hbm, hbm, hbm],
        out_specs=vmem,
        scratch_shapes=[
            pltpu.VMEM(traces.shape, BF16),
            pltpu.VMEM(ray_phase.shape, BF16),
            pltpu.VMEM(beam_basis.shape, BF16),
            pltpu.SMEM((shots,), jnp.int32),
            pltpu.VMEM((slabs, beams) + block, jnp.int32),
            pltpu.VMEM((beams * WIN_OWN, 1, slabs * depths), jnp.int32),
            pltpu.VMEM((beams * WIN_OWN, ray_phase.shape[0], wide), F32),
            pltpu.VMEM((2, chips, slabs, rows, wide), F32),
            pltpu.VMEM((chips, slabs, rows, wide), F32),
            pltpu.VMEM((slabs, hops, rows, wide), BF16),
            pltpu.VMEM((slabs, hops, rows, wide), BF16),
            pltpu.VMEM((slabs, rows, wide), BF16),
            pltpu.VMEM((slabs, rows, wide), BF16),
            pltpu.VMEM((chips, depths, lateral), F32),
            pltpu.VMEM((chips, depths, lateral), F32),
            pltpu.VMEM((hops, 2 * depths, lateral // 2), BF16),
            pltpu.VMEM((hops, 2 * depths, lateral // 2), BF16),
            dma(()), dma(()), dma(()),
            dma((beams,)), dma((beams,)),
            dma((slabs,)), dma((slabs,)),
            dma((chips,)), dma((chips,)),
            dma((slabs, hops)), dma((slabs, hops)),
            dma((slabs,)), dma((slabs,)),
            dma((chips,)), dma((chips,)),
            dma((hops,)), dma((hops,)),
        ],
        compiler_params=pltpu.CompilerParams(
            collective_id=0, has_side_effects=True, vmem_limit_bytes=56 * 1024 * 1024
        ),
        name="migrate",
    )(
        shot_window, trace_slot.reshape(shots, 1, per_shot), ray_index, slant_matrix(scale),
        traces, ray_phase, beam_basis,
    )


def solution(mesh):
    in_specs = (
        P(("slab", "beam"), None, None),
        P(("slab", "beam")),
        P(("slab", "beam"), None),
        P(),
        P("beam", "slab"),
        P(None, "beam", None),
    )
    out_specs = P("slab", "beam")
    return jax.shard_map(body, mesh=mesh, in_specs=in_specs, out_specs=out_specs, check_vma=False)
```

```python
import functools

import jax
import jax.numpy as jnp
import numpy as np
from jax import lax
from jax.experimental import pallas as pl
from jax.experimental.pallas import tpu as pltpu
from jax.sharding import PartitionSpec as P

P_SIZE = 64
K = 64
WIN_OWN = 4
MESH = pl.DeviceIdType.MESH
F32 = jnp.float32
BF16 = jnp.bfloat16


def slant_matrix(scale):
    steps = np.arange(K)[:, None] * np.arange(P_SIZE)[None, :] % K
    c = np.cos(2.0 * np.pi * steps / K) * scale
    d = np.sin(2.0 * np.pi * steps / K) * scale
    return np.block([[c, d], [d, -c]]).astype(np.float32)


def migrate_kernel(
    slabs, beams, window_ref, slot_ref, index_ref, slant, traces_hbm, table_hbm, basis_hbm, out_ref,
    traces, table, basis, order, gathered, index_rows, products, waves,
    core_in, chip_out, chip_in, slab_out, slab_in, part_out, part_in, edge_out, edge_in,
    table_sem, traces_sem, basis_sem, ib_s, ib_r, is_s, is_r,
    core_s, core_r, chip_s, chip_r, slab_s, slab_r, part_s, part_r, edge_s, edge_r,
):
    chips = beams // 2
    slab, beam = lax.axis_index("slab"), lax.axis_index("beam")
    core, chip = lax.rem(beam, 2), lax.div(beam, 2)
    other = 1 - core
    sibling = (slab, 2 * chip + other)
    chip_of = [lax.rem(chip + j, chips) for j in range(chips)]
    slab_of = [lax.rem(slab + k, slabs) for k in range(1, slabs)] + [slab]
    beam_peers = [(slab, lax.rem(beam + j, beams)) for j in range(1, beams)]
    slab_peers = [(s, beam) for s in slab_of[:-1]]

    load_table = pltpu.make_async_copy(table_hbm, table, table_sem)
    load_traces = pltpu.make_async_copy(traces_hbm, traces, traces_sem)
    load_basis = pltpu.make_async_copy(basis_hbm, basis, basis_sem)
    load_traces.start()
    load_table.start()
    barrier = pltpu.get_barrier_semaphore()
    for peer in beam_peers + slab_peers:
        pl.semaphore_signal(barrier, inc=1, device_id=peer, device_id_type=MESH)

    def send(src, dst, send_sem, recv_sem, device):
        copy = pltpu.make_async_remote_copy(
            src_ref=src, dst_ref=dst, send_sem=send_sem, recv_sem=recv_sem,
            device_id=device, device_id_type=MESH,
        )
        copy.start()
        return copy

    own_rows, depths = index_ref.shape
    gathered[slab, beam] = jnp.zeros(gathered.shape[2:], jnp.int32)
    gathered[slab, beam, :own_rows, :depths] = index_ref[...]
    shots, per_shot, doubled = traces.shape
    per_owner = shots // beams
    counts = [jnp.int32(0)] * beams
    places = []
    for i in range(shots):
        owner = lax.div(window_ref[i], WIN_OWN)
        place = jnp.int32(0)
        for b in range(beams):
            hit = owner == b
            place = jnp.where(hit, b * per_owner + counts[b], place)
            counts[b] = jnp.where(hit, counts[b] + 1, counts[b])
        places.append(place)
    for m in range(shots):
        shot = jnp.int32(0)
        for i in range(shots):
            shot = jnp.where(places[i] == m, jnp.int32(i), shot)
        order[m] = shot
    pl.semaphore_wait(barrier, len(beam_peers) + len(slab_peers))
    first = [
        send(gathered.at[slab, beam], gathered.at[slab, beam], ib_s.at[j], ib_r.at[j], peer)
        for j, peer in enumerate(beam_peers)
    ]

    half_f = doubled // 2
    slot_rows = lax.broadcasted_iota(jnp.int32, (K, per_shot), 0)

    def bin_shot(m, carry):
        shot = order[m]
        pick = (slot_rows == slot_ref[shot]).astype(F32).astype(BF16)
        binned = jnp.dot(pick, traces[shot], preferred_element_type=F32)
        re, im = binned[:, :half_f], binned[:, half_f:]
        both = jnp.concatenate(
            [jnp.concatenate([re, -im], axis=1), jnp.concatenate([im, re], axis=1)], axis=0
        )
        high = both.astype(BF16)
        low = (both - high.astype(F32)).astype(BF16)
        parts = lax.dot_general(
            table[...],
            jnp.concatenate([high, low], axis=0),
            (((1,), (1,)), ((), ())),
            preferred_element_type=F32,
        )
        part = parts[:, : 2 * K] + parts[:, 2 * K :]
        base = lax.div(m, per_owner) * WIN_OWN
        for v in range(WIN_OWN):
            weight = jnp.where(window_ref[shot] == base + v, 1.0, 0.0)
            products[base + v] += weight * part
        return carry

    products[...] = jnp.zeros(products.shape, F32)
    load_table.wait()
    load_traces.wait()
    load_basis.start()
    lax.fori_loop(0, shots // 4, bin_shot, 0, unroll=4)
    for copy in first:
        copy.wait()
    second = [
        send(gathered.at[slab], gathered.at[slab], is_s.at[k], is_r.at[k], peer)
        for k, peer in enumerate(slab_peers)
    ]
    lax.fori_loop(shots // 4, shots, bin_shot, 0, unroll=4)
    for copy in second:
        copy.wait()
    for b in range(beams):
        line = jnp.concatenate([gathered[s, b][:own_rows, :depths] for s in range(slabs)], axis=1)
        for w in range(WIN_OWN):
            index_rows[b * WIN_OWN + w] = line[w : w + 1]

    ray_rows = lax.broadcasted_iota(jnp.int32, (table.shape[0], slabs * depths), 0)

    def owner_waves(x, c):
        owner = 2 * x + c
        for v in range(WIN_OWN):
            w = owner * WIN_OWN + v
            pick = (ray_rows == index_rows[w]).astype(F32).astype(BF16)
            value = products[w]
            high = value.astype(BF16)
            low = (value - high.astype(F32)).astype(BF16)
            parts = lax.dot_general(
                pick,
                jnp.concatenate([high, low], axis=1),
                (((0,), (0,)), ((), ())),
                preferred_element_type=F32,
            )
            part = parts[:, : 2 * K] + parts[:, 2 * K :]
            for s in range(slabs):
                waves[c, x, s, v * depths : (v + 1) * depths, :] = (
                    part[s * depths : (s + 1) * depths]
                )

    core_copies = {}
    chip_copies = [[] for _ in slab_of]
    for j in list(range(1, chips)) + [0]:
        x = chip_of[j]
        owner_waves(x, other)
        core_copies[j] = send(
            waves.at[other, x], core_in.at[j], core_s.at[j], core_r.at[j], sibling
        )
        owner_waves(x, core)
        core_copies[j].wait_recv()
        if j == 0:
            continue
        for k, s in enumerate(slab_of):
            chip_out[k, j - 1] = (waves[core, x, s] + core_in[j, s]).astype(BF16)
            chip_copies[k].append(
                send(
                    chip_out.at[k, j - 1], chip_in.at[k, j - 1],
                    chip_s.at[k, j - 1], chip_r.at[k, j - 1], (slab, 2 * x + core),
                )
            )
    slab_copies = []
    total = None
    for k, s in enumerate(slab_of):
        total = waves[core, chip, s] + core_in[0, s]
        for j, copy in enumerate(chip_copies[k]):
            copy.wait_recv()
            total = total + chip_in[k, j].astype(F32)
        if k < slabs - 1:
            slab_out[k] = total.astype(BF16)
            slab_copies.append(
                send(slab_out.at[k], slab_in.at[k], slab_s.at[k], slab_r.at[k], (s, beam))
            )
    for k, copy in enumerate(slab_copies):
        copy.wait_recv()
        total = total + slab_in[k].astype(F32)
    wave = jnp.dot(
        total, slant[...], precision=lax.Precision.HIGHEST, preferred_element_type=F32
    )
    lateral = out_ref.shape[1]
    rows = [wave[w * depths : (w + 1) * depths] for w in range(WIN_OWN)]
    mixed = []
    for lo in (0, P_SIZE):
        part = jnp.concatenate([r[:, lo : lo + P_SIZE] for r in rows], axis=1)
        high = part.astype(BF16)
        low = (part - high.astype(F32))
        mixed.append(jnp.concatenate([high.astype(F32), low], axis=0).astype(BF16))
    load_basis.wait()

    def terms(owner):
        cols = pl.ds(pl.multiple_of(owner * lateral, lateral), lateral)
        both = jnp.dot(mixed[0], basis[0, :, cols], preferred_element_type=F32)
        both += jnp.dot(mixed[1], basis[1, :, cols], preferred_element_type=F32)
        return both[:depths] + both[depths:]

    order = list(range(1, chips)) + [0]
    part_copies = {}
    for j in order:
        part_out[j] = terms(2 * chip_of[j] + other)
        part_copies[j] = send(
            part_out.at[j], part_in.at[j], part_s.at[j], part_r.at[j], sibling
        )
    edge_copies = []
    half = lateral // 2
    for j in range(1, chips):
        value = terms(2 * chip_of[j] + core)
        part_copies[j].wait_recv()
        value = value + part_in[j]
        edge_out[j - 1] = jnp.concatenate([value[:, :half], value[:, half:]], axis=0).astype(BF16)
        edge_copies.append(
            send(
                edge_out.at[j - 1], edge_in.at[j - 1], edge_s.at[j - 1], edge_r.at[j - 1],
                (slab, 2 * chip_of[j] + core),
            )
        )
    value = terms(beam)
    part_copies[0].wait_recv()
    out_ref[...] = value + part_in[0]
    for j, copy in enumerate(edge_copies):
        copy.wait_recv()
        edge = edge_in[j].astype(F32)
        out_ref[:, :half] += edge[:depths]
        out_ref[:, half:] += edge[depths:]
    sent = list(core_copies.values()) + slab_copies + list(part_copies.values()) + edge_copies
    for row in chip_copies:
        sent += row
    for copy in sent:
        copy.wait_send()


def body(traces, shot_window, trace_slot, ray_phase, ray_index, beam_basis):
    shots, per_shot, doubled = traces.shape
    beams = lax.axis_size("beam")
    slabs = lax.axis_size("slab")
    scale = (shots * slabs * beams * per_shot / (WIN_OWN * beams)) ** (-0.5)
    own_rows, depths = ray_index.shape
    chips = beams // 2
    lateral = beam_basis.shape[2] // beams
    rows = WIN_OWN * depths
    wide = 2 * K
    hops = max(chips - 1, 1)
    vmem = pl.BlockSpec(memory_space=pltpu.VMEM)
    smem = pl.BlockSpec(memory_space=pltpu.SMEM)
    hbm = pl.BlockSpec(memory_space=pl.ANY)
    dma = pltpu.SemaphoreType.DMA
    block = (-(-own_rows // 8) * 8, -(-depths // 128) * 128)
    return pl.pallas_call(
        functools.partial(migrate_kernel, slabs, beams),
        out_shape=jax.ShapeDtypeStruct((depths, lateral), F32),
        in_specs=[smem, vmem, vmem, vmem, hbm, hbm, hbm],
        out_specs=vmem,
        scratch_shapes=[
            pltpu.VMEM(traces.shape, BF16),
            pltpu.VMEM(ray_phase.shape, BF16),
            pltpu.VMEM(beam_basis.shape, BF16),
            pltpu.SMEM((shots,), jnp.int32),
            pltpu.VMEM((slabs, beams) + block, jnp.int32),
            pltpu.VMEM((beams * WIN_OWN, 1, slabs * depths), jnp.int32),
            pltpu.VMEM((beams * WIN_OWN, ray_phase.shape[0], wide), F32),
            pltpu.VMEM((2, chips, slabs, rows, wide), F32),
            pltpu.VMEM((chips, slabs, rows, wide), F32),
            pltpu.VMEM((slabs, hops, rows, wide), BF16),
            pltpu.VMEM((slabs, hops, rows, wide), BF16),
            pltpu.VMEM((slabs, rows, wide), BF16),
            pltpu.VMEM((slabs, rows, wide), BF16),
            pltpu.VMEM((chips, depths, lateral), F32),
            pltpu.VMEM((chips, depths, lateral), F32),
            pltpu.VMEM((hops, 2 * depths, lateral // 2), BF16),
            pltpu.VMEM((hops, 2 * depths, lateral // 2), BF16),
            dma(()), dma(()), dma(()),
            dma((beams,)), dma((beams,)),
            dma((slabs,)), dma((slabs,)),
            dma((chips,)), dma((chips,)),
            dma((slabs, hops)), dma((slabs, hops)),
            dma((slabs,)), dma((slabs,)),
            dma((chips,)), dma((chips,)),
            dma((hops,)), dma((hops,)),
        ],
        compiler_params=pltpu.CompilerParams(
            collective_id=0, has_side_effects=True, vmem_limit_bytes=56 * 1024 * 1024
        ),
        name="migrate",
    )(
        shot_window, trace_slot.reshape(shots, 1, per_shot), ray_index, slant_matrix(scale),
        traces, ray_phase, beam_basis,
    )


def solution(mesh):
    in_specs = (
        P(("slab", "beam"), None, None),
        P(("slab", "beam")),
        P(("slab", "beam"), None),
        P(),
        P("beam", "slab"),
        P(None, "beam", None),
    )
    out_specs = P("slab", "beam")
    return jax.shard_map(body, mesh=mesh, in_specs=in_specs, out_specs=out_specs, check_vma=False)
```
